256 devices in a mesh: req: 8 (over x, core), ctx: 32 (over y, z).
Axes of the slice: x: 4, y: 4, z: 8, core: 2. Of those that a mesh axis runs over, the one named last changes fastest.
Arguments:
- suffix_hidden: bfloat16 [8, 2048, 7168], P('req', 'ctx'), may hold values from -6 to 6
- kv_down: bfloat16 [7168, 576], P('ctx'), may hold values from -0.0625 to 0.0625
- kv_gain: float32 [512], replicated, may hold values from 0.25 to 1.75
- queries: bfloat16 [8, 2048, 64, 576], P('req', 'ctx'), may hold values from -300 to 300
- pool: bfloat16 [96, 32, 576], P('req', 'ctx'), may hold values from -4 to 4
- hit_holder: int32 [8, 8], replicated, may hold values from 0 to 7, as said below
- hit_slot: int32 [8, 8], replicated, may hold values from 0 to 11, as said below
- hit_count: int32 [8], replicated, may hold values from 4 to 8, as said below
Outputs:
- attended: bfloat16 [8, 2048, 64, 512], P('req', 'ctx')
The draws below stay inside these ranges and needn't reach their ends.
Inputs may be any that keep to these rules, and one draw needn't show every extreme that they name: `hit_holder`: entry j of request r is used when j < hit_count[r]. Of one request's used entries at most 2 name the same holder, and some request has 2 on one holder. Unused entries are in range and ignored. `hit_slot`: two used entries of one request never name the same holder and place. `hit_count`: some request has 8.
All inputs are finite; a program needn't handle non-finite values.
Results may differ from the reference program's by a relative error of at most 0.0065.
Values may be sent and summed in bfloat16 or wider, within the bound.
No kernel may reach another device: no remote copies, remote signals or barrier semaphores. Data moves between devices by JAX's collectives and lax.ppermute only.
A program may use at most 64 MiB of HBM per device.

```python
import jax
import jax.numpy as jnp
from jax import lax

D = 7168
H = 64
KVR = 512
PAGE = 32
CMAX = 8
CAP = 2
POOL_DEV = 12
Q_DEV = 64
LAT = 576
REQS = 8
SUF = 2048
POOL = 96


def page_routes(key):
    route_key = jax.random.fold_in(key, 31)
    cells = REQS * CAP

    def one_list(list_key):
        parts_keys = jax.random.split(list_key, 4)
        full_row = jax.random.randint(parts_keys[0], (), 0, REQS)
        ranks = jax.random.permutation(parts_keys[1], cells)
        cell_ids = jnp.arange(cells, dtype=jnp.int32)
        scores = jnp.where(cell_ids // CAP == full_row, ranks - cells, ranks)
        chosen = jnp.argsort(scores, stable=True)[:CMAX]
        chosen = chosen[jax.random.permutation(parts_keys[2], CMAX)]
        holder = (chosen // CAP).astype(jnp.int32)
        place = jax.random.randint(parts_keys[3], (CMAX,), 0, POOL_DEV // CAP) * CAP + chosen % CAP
        return (holder, place.astype(jnp.int32))
    holders, places = jax.vmap(one_list)(jax.random.split(route_key, REQS))
    counts = jax.random.randint(jax.random.fold_in(route_key, 7), (REQS,), CMAX // 2, CMAX + 1)
    fullest = jax.random.randint(jax.random.fold_in(route_key, 9), (), 0, REQS)
    counts = jnp.where(jnp.arange(REQS) == fullest, CMAX, counts).astype(jnp.int32)
    return (holders, places, counts)


def pool_base(key):
    base = jax.random.normal(jax.random.fold_in(key, 21), (POOL, PAGE, LAT), jnp.float32)
    return jnp.clip(base, -4.0, 4.0)


def draw_hit_holder(key, part):
    routes = page_routes(key)
    return routes[0]


def draw_hit_slot(key, part):
    routes = page_routes(key)
    return routes[1]


def draw_hit_count(key, part):
    routes = page_routes(key)
    return routes[2]


def draw_pool(key, part):
    base = pool_base(key)
    return base.astype(jnp.bfloat16)


def draw_queries(key, part):
    key = jax.random.fold_in(key, 5)
    shape = (REQS, SUF, H, LAT)
    values = jnp.clip(jax.random.normal(key, shape, jnp.float32) * 1.25, -7.5, 7.5)
    return values.astype(jnp.bfloat16)


def block_levels(own_key, dims, cuts, least, largest):
    def one(position, shards_of):
        steps = jax.random.uniform(jax.random.fold_in(jax.random.fold_in(own_key, 6), position), (shards_of,), jnp.float32, least / len(cuts), largest / len(cuts))
        return jnp.repeat(jnp.exp(steps), dims[position] // shards_of).reshape((-1,) + (1,) * (len(dims) - position - 1))

    loudness = one(*cuts[0])
    for cut in cuts[1:]:
        loudness = loudness * one(*cut)
    return loudness


def centred(key, dims, deviation, most, cuts=(), kind=jnp.bfloat16):
    entries = jax.random.normal(key, dims, jnp.float32) * deviation
    if len(cuts) > 0:
        entries = block_levels(key, dims, cuts, -0.22, 0.18) * entries
    return jnp.clip(entries, min=-most, max=most).astype(kind)


def setup_inputs(seed: int = 0) -> dict:
    arg_keys = jax.random.split(jax.random.key(seed), 9)
    return {
        "suffix_hidden": centred(arg_keys[0], (REQS, SUF, D), 1.0, 6.0, ((0, 8), (1, 32))),
        "kv_down": centred(arg_keys[1], (D, LAT), D ** -0.5, 0.0625, ((0, 32),)),
        "kv_gain": jnp.clip(1.0 + 0.15 * jax.random.normal(arg_keys[2], (KVR,), jnp.float32), 0.25, 1.75),
        "queries": draw_queries(jax.random.fold_in(arg_keys[8], 71), 0),
        "pool": draw_pool(jax.random.fold_in(arg_keys[8], 71), 0),
        "hit_holder": draw_hit_holder(jax.random.fold_in(arg_keys[8], 71), 0),
        "hit_slot": draw_hit_slot(jax.random.fold_in(arg_keys[8], 71), 0),
        "hit_count": draw_hit_count(jax.random.fold_in(arg_keys[8], 71), 0),
    }


score_scale = 192.0 ** (-0.5)
rope_base = 10000.0
norm_eps = 1e-06

def rotate(rope_part, positions):
    half = rope_part.shape[1] // 2
    steps = jnp.arange(half, dtype=jnp.float32) * (2.0 / rope_part.shape[1])
    freqs = jnp.exp(-steps * jnp.log(rope_base))
    angles = positions[:, None] * freqs[None, :]
    cosine = jnp.cos(angles)
    sine = jnp.sin(angles)
    first = rope_part[:, :half]
    second = rope_part[:, half:]
    return jnp.concatenate([first * cosine - second * sine, second * cosine + first * sine], 1)

def finish_keys(latent, kv_gain, start):
    width = kv_gain.shape[0]
    compressed = latent[:, :width]
    mean_square = lax.optimization_barrier(jnp.mean(compressed * compressed, axis=1, keepdims=True))
    normed = compressed * lax.rsqrt(mean_square + norm_eps) * kv_gain
    positions = (start + jnp.arange(latent.shape[0], dtype=jnp.int32)).astype(jnp.float32)
    return jnp.concatenate([normed, rotate(latent[:, width:], positions)], 1).astype(jnp.bfloat16)

def reference(suffix_hidden, kv_down, kv_gain, queries, pool, hit_holder, hit_slot, hit_count):
    cache_tokens = CMAX * PAGE
    token_page = jnp.arange(cache_tokens, dtype=jnp.int32) // PAGE
    suffix_ids = jnp.arange(SUF, dtype=jnp.int32)

    def one_request(operands):
        hidden, query, holder, place, count = operands
        latent = jnp.dot(hidden, kv_down, preferred_element_type=jnp.float32)
        fresh = finish_keys(latent, kv_gain, count * PAGE)
        pages = jnp.take(pool, holder * POOL_DEV + place, axis=0).reshape(cache_tokens, LAT)
        keys = jnp.concatenate([pages, fresh], 0).astype(jnp.float32)
        values = keys[:, :KVR]
        cached_ok = token_page < count

        def one_block(block_ops):
            block, first = block_ops
            scores = jnp.einsum('thd,kd->thk', block.astype(jnp.float32), keys) * score_scale
            query_pos = first + jnp.arange(Q_DEV, dtype=jnp.int32)
            causal = suffix_ids[None, :] <= query_pos[:, None]
            allowed = jnp.concatenate([jnp.broadcast_to(cached_ok[None, :], (Q_DEV, cache_tokens)), causal], 1)[:, None, :]
            peak = lax.optimization_barrier(jnp.max(jnp.where(allowed, scores, -1e+30), axis=2, keepdims=True))
            weights = jnp.where(allowed, jnp.exp(scores - peak), 0.0)
            total = lax.optimization_barrier(jnp.sum(weights, axis=2, keepdims=True))
            rounded = lax.optimization_barrier(weights.astype(jnp.bfloat16))
            mixed = jnp.einsum('thk,kc->thc', rounded.astype(jnp.float32), values)
            return (mixed / total).astype(jnp.bfloat16)
        blocks = query.reshape(SUF // Q_DEV, Q_DEV, H, LAT)
        firsts = jnp.arange(SUF // Q_DEV, dtype=jnp.int32) * Q_DEV
        return lax.map(one_block, (blocks, firsts)).reshape(SUF, H, KVR)
    return lax.map(one_request, (suffix_hidden, queries, hit_holder, hit_slot, hit_count))
```

```python
import functools
import math

import jax
import jax.numpy as jnp
from jax import lax
from jax.experimental import pallas as pl
from jax.experimental.pallas import tpu as pltpu
from jax.sharding import PartitionSpec as P

PAGE = 32
CAP = 2
score_scale = 192.0 ** (-0.5)
rope_base = 10000.0
norm_eps = 1e-06
exp2_scale = score_scale * math.log2(math.e)
masked = -1e30

REQ, Y, Z = 8, 4, 8
SLICE = 32
WORKERS = 7
TOK = 64
HEADS = 64
LAT = 576
VAL = 512
AUG = LAT + TOK

Z_GROUPS = [[y * Z + z for z in range(Z)] for y in range(Y)]
X_GROUPS = [[2 * x + core for x in range(REQ // 2)] for core in range(2)]


def y_shift(d):
    return [(i, (i + Z * d) % (Y * Z)) for i in range(Y * Z)]


def mm(a, b):
    return jnp.dot(a, b, preferred_element_type=jnp.float32)


def partial_kernel(info, h_ref, *refs):
    kv_refs, (keep_ref, give_ref) = refs[:Y], refs[Y:]
    y, core = info[0], info[1]
    for half, out in ((core, keep_ref), (1 - core, give_ref)):
        total = None
        for d in range(Y):
            at = pl.multiple_of(lax.rem(y + Y - d, Y) * (Z * SLICE), Z * SLICE)
            rows = [h_ref[2 * j + half, :, pl.ds(at, Z * SLICE)] for j in range(REQ // 2)]
            term = mm(jnp.concatenate(rows, 0), kv_refs[d][...])
            total = term if total is None else total + term
        out[...] = total.reshape(out.shape)


def partial_latents(info, hidden, kvs):
    shape = jax.ShapeDtypeStruct((REQ // 2, TOK, LAT), jnp.float32)
    vmem = pl.BlockSpec(memory_space=pltpu.VMEM)
    return pl.pallas_call(
        partial_kernel,
        in_specs=[pl.BlockSpec(memory_space=pltpu.SMEM)] + [vmem] * (1 + Y),
        out_specs=[vmem, vmem],
        out_shape=[shape, shape],
        compiler_params=pltpu.CompilerParams(vmem_limit_bytes=24 * 2**20),
        name="partial_latents",
    )(info, hidden, *kvs)


def finish_kernel(parts_ref, gain_ref, cos_ref, sin_ref, out_ref):
    latent = parts_ref[0]
    for x in range(1, REQ // 2):
        latent = latent + parts_ref[x]
    compressed = latent[:, :VAL]
    mean_square = jnp.mean(compressed * compressed, axis=1, keepdims=True)
    normed = compressed * lax.rsqrt(mean_square + norm_eps) * gain_ref[...]
    half = (LAT - VAL) // 2
    first, second = latent[:, VAL : VAL + half], latent[:, VAL + half :]
    cosine, sine = cos_ref[...], sin_ref[...]
    keys = jnp.concatenate(
        [normed, first * cosine - second * sine, second * cosine + first * sine], 1
    ).astype(jnp.bfloat16)
    for z in range(Z):
        out_ref[z] = keys


def finish_keys(parts, gain, cosine, sine):
    vmem = pl.BlockSpec(memory_space=pltpu.VMEM)
    return pl.pallas_call(
        finish_kernel,
        in_specs=[vmem] * 4,
        out_specs=vmem,
        out_shape=jax.ShapeDtypeStruct((Z, TOK, LAT), jnp.bfloat16),
        name="finish_keys",
    )(parts, gain, cosine, sine)


def attend_kernel(sub, blocks, bias_of, carry, final, info, *refs):
    q_ref, ahead_ref = refs[:2]
    refs = refs[2:]
    if carry:
        acc_ref, stat_ref = refs[:2]
        refs = refs[2:]
    k_refs, refs = refs[:blocks], refs[blocks:]
    outs, (kt, s_even, s_odd) = refs[:-3], refs[-3:]
    step = pl.program_id(0)
    tile = q_ref.shape[0]
    subs = tile // sub
    scores = (s_even, s_odd)

    def product(rows, row0):
        token = (row0 + lax.broadcasted_iota(jnp.int32, (sub, TOK), 0)) // HEADS
        place = lax.broadcasted_iota(jnp.int32, (sub, TOK), 1)
        mark = jnp.where(token == place, 1.0, 0.0).astype(jnp.bfloat16)
        return mm(jnp.concatenate([rows, mark], 1), kt[...])

    @pl.when(step == 0)
    def prepare():
        at = 0
        for n, k in enumerate(k_refs):
            size = k.shape[0]
            kt[:LAT, at : at + size] = k[...].T
            kt[LAT:, at : at + size] = bias_of(info, n, size).astype(jnp.bfloat16)
            at += size
        s_even[...] = product(q_ref[:sub, :], 0)

    for s in range(subs):
        here, later = scores[s % 2], scores[(s + 1) % 2]
        if s + 1 < subs:
            rows = q_ref[(s + 1) * sub : (s + 2) * sub, :]
        else:
            rows = ahead_ref[...]
        later[...] = product(rows, step * tile + (s + 1) * sub)
        at = slice(s * sub, (s + 1) * sub)
        score = here[...]
        peak = jnp.max(score, axis=1, keepdims=True)
        if carry:
            stat = stat_ref[at, :]
            old_peak, old_total = stat[:, :1], stat[:, 64:65]
            peak = jnp.maximum(peak, old_peak)
        shift = peak * exp2_scale
        weights = jnp.exp2(score * exp2_scale - shift)
        total = jnp.sum(weights, axis=1, keepdims=True)
        rounded = weights.astype(jnp.bfloat16)
        accum, place = None, 0
        for k in k_refs:
            size = k.shape[0]
            term = mm(rounded[:, place : place + size], k[:, :VAL])
            accum = term if accum is None else accum + term
            place += size
        if carry:
            factor = jnp.exp2(old_peak * exp2_scale - shift)
            total = total + old_total * factor
            accum = accum + acc_ref[at, :] * factor
        if final:
            outs[0][at, :] = (accum / total).astype(jnp.bfloat16)
        else:
            outs[0][at, :] = accum
            outs[1][at, :] = jnp.concatenate(
                [jnp.broadcast_to(peak, (sub, 64)), jnp.broadcast_to(total, (sub, 64))], 1
            )


def attend(info, queries, carry, keys, bias_of, final, tile=1024, sub=256):
    rows = queries.shape[0]
    steps, subs = rows // tile, tile // sub
    total = sum(k.shape[0] for k in keys)
    row = lambda width: pl.BlockSpec((tile, width), lambda i, s: (i, 0))
    ahead = pl.BlockSpec((sub, LAT), lambda i, s: (jnp.minimum((i + 1) * subs, rows // sub - 1), 0))
    whole = lambda a: pl.BlockSpec(a.shape, lambda i, s: (0, 0))
    carry = [] if carry is None else list(carry)
    if final:
        shapes = [jax.ShapeDtypeStruct((rows, VAL), jnp.bfloat16)]
        out_specs = [row(VAL)]
    else:
        shapes = [
            jax.ShapeDtypeStruct((rows, VAL), jnp.float32),
            jax.ShapeDtypeStruct((rows, 128), jnp.float32),
        ]
        out_specs = [row(VAL), row(128)]
    return pl.pallas_call(
        functools.partial(attend_kernel, sub, len(keys), bias_of, bool(carry), final),
        grid_spec=pltpu.PrefetchScalarGridSpec(
            num_scalar_prefetch=1,
            grid=(steps,),
            in_specs=[row(LAT), ahead]
            + [row(VAL), row(128)][: len(carry)]
            + [whole(k) for k in keys],
            out_specs=out_specs,
            scratch_shapes=[
                pltpu.VMEM((AUG, total), jnp.bfloat16),
                pltpu.VMEM((sub, total), jnp.float32),
                pltpu.VMEM((sub, total), jnp.float32),
            ],
        ),
        out_shape=shapes,
        compiler_params=pltpu.CompilerParams(vmem_limit_bytes=44 * 2**20),
        cost_estimate=pl.CostEstimate(
            flops=2 * rows * total * (LAT + VAL),
            bytes_accessed=rows * 2048,
            transcendentals=rows * total,
        ),
        name="attend_last" if final else "attend_first",
    )(info, queries, queries, *carry, *keys)


def near_bias(info, n, size):
    key = lax.broadcasted_iota(jnp.int32, (TOK, size), 1)
    token = lax.broadcasted_iota(jnp.int32, (TOK, size), 0)
    if n == 0:
        allowed = lax.rem(key, 8) < info[2]
    else:
        allowed = key <= info[1] * TOK + token
    return jnp.where(allowed, 0.0, masked)


def far_bias(info, n, size):
    bias = jnp.where(info[0] >= n + 1, 0.0, masked)
    return jnp.full((TOK, size), bias, jnp.float32)


def shards(suffix_hidden, kv_down, kv_gain, queries, pool, hit_holder, hit_slot, hit_count):
    req = lax.axis_index("req")
    ctx = lax.axis_index("ctx")
    y, z = ctx // Z, ctx % Z
    count = lax.dynamic_index_in_dim(hit_count, req, 0, keepdims=False)

    hidden = suffix_hidden[0].reshape(TOK, Y * Z, WORKERS, SLICE)
    hidden = hidden.transpose(2, 0, 1, 3).reshape(WORKERS, TOK, Y * Z * SLICE)
    hidden = jnp.concatenate([hidden, jnp.zeros((REQ - WORKERS,) + hidden.shape[1:], hidden.dtype)], 0)
    hidden = lax.all_to_all(hidden, "req", 0, 0)

    piece = lax.dynamic_slice(
        kv_down, (jnp.minimum(req, WORKERS - 1) * SLICE, 0), (SLICE, LAT)
    )
    row = lax.all_to_all(
        jnp.broadcast_to(piece[None], (Z, SLICE, LAT)), "ctx", 0, 0, axis_index_groups=Z_GROUPS
    ).reshape(Z * SLICE, LAT)
    kvs = [row] + [lax.ppermute(row, "ctx", y_shift(d)) for d in (1, 2, 3)]

    keep, give = partial_latents(jnp.stack([y, req % 2]), hidden, kvs)
    swapped = lax.ppermute(give, "req", [(i, i ^ 1) for i in range(REQ)])
    parts = lax.all_to_all(keep + swapped, "req", 0, 0, axis_index_groups=X_GROUPS)

    half = (LAT - VAL) // 2
    steps = jnp.arange(half, dtype=jnp.float32) * (2.0 / (LAT - VAL))
    freqs = jnp.exp(-steps * jnp.log(rope_base))
    first = count * PAGE + ctx * TOK
    positions = (first + jnp.arange(TOK, dtype=jnp.int32)).astype(jnp.float32)
    angles = positions[:, None] * freqs[None, :]
    fresh = finish_keys(parts, kv_gain[None], jnp.cos(angles), jnp.sin(angles))

    entries = jnp.arange(hit_holder.shape[1], dtype=jnp.int32)
    used = entries[None, :] < hit_count[:, None]
    earlier = (
        (hit_holder[:, :, None] == hit_holder[:, None, :])
        & used[:, None, :]
        & (entries[None, None, :] < entries[None, :, None])
    )
    rank = jnp.sum(earlier.astype(jnp.int32), axis=2)
    cap_ids = jnp.arange(CAP, dtype=jnp.int32)
    pick = (
        used[:, None, :]
        & (hit_holder[:, None, :] == req)
        & (rank[:, None, :] == cap_ids[None, :, None])
    )
    place = jnp.sum(jnp.where(pick, hit_slot[:, None, :], 0), axis=2)
    outgoing = jnp.take(pool[:, 0], place.reshape(-1), axis=0).reshape(REQ, CAP, LAT)
    incoming = lax.all_to_all(outgoing, "req", 0, 0).reshape(REQ * CAP, LAT)
    holder = lax.dynamic_index_in_dim(hit_holder, req, 0, keepdims=False)
    my_rank = lax.dynamic_index_in_dim(rank, req, 0, keepdims=False)
    cached = jnp.take(incoming, holder * CAP + jnp.minimum(my_rank, CAP - 1), axis=0)
    cached, kvs[3] = lax.optimization_barrier((cached, kvs[3]))
    cached = lax.all_to_all(
        jnp.broadcast_to(cached[None], (Y * Z,) + cached.shape), "ctx", 0, 0
    ).reshape(-1, LAT)

    near = lax.all_to_all(fresh, "ctx", 0, 0, axis_index_groups=Z_GROUPS).reshape(-1, LAT)
    far = [lax.ppermute(near, "ctx", y_shift(d)) for d in (1, 2, 3)]

    info = jnp.stack([y, z, count]).astype(jnp.int32)
    rows = queries[0].reshape(-1, LAT)
    carry = attend(info, rows, None, [cached, near], near_bias, False)
    (out,) = attend(info, rows, carry, far, far_bias, True)
    return out.reshape(1, TOK, HEADS, VAL)


def solution(mesh):
    in_specs = (
        P("req", "ctx", None),
        P("ctx", None),
        P(),
        P("req", "ctx", None, None),
        P("req", "ctx", None),
        P(),
        P(),
        P(),
    )
    out_specs = P("req", "ctx", None, None)
    return jax.shard_map(shards, mesh=mesh, in_specs=in_specs, out_specs=out_specs, check_vma=False)
```

```python
import functools
import math

import jax
import jax.numpy as jnp
from jax import lax
from jax.experimental import pallas as pl
from jax.experimental.pallas import tpu as pltpu
from jax.sharding import PartitionSpec as P

PAGE = 32
CAP = 2
score_scale = 192.0 ** (-0.5)
rope_base = 10000.0
norm_eps = 1e-06
exp2_scale = score_scale * math.log2(math.e)
masked = -1e30

REQ, X, Y, Z = 8, 4, 4, 8
SLICE = 32
WORKERS = 7
TOK = 64
HEADS = 64
LAT = 576
VAL = 512
AUG = 640
DEVICE_LANE, PAGE_LANE = LAT, LAT + Y * Z

Z_GROUPS = [[y * Z + z for z in range(Z)] for y in range(Y)]


def y_shift(d):
    return [(i, (i + Z * d) % (Y * Z)) for i in range(Y * Z)]


def mm(a, b):
    return jnp.dot(a, b, preferred_element_type=jnp.float32)


def cut_kernel(info, h_ref, *refs):
    out_refs, staged = refs[:X], refs[X]
    x = info[0]
    per = 4
    half = Y * Z * SLICE
    staged[x ^ (X - 1), :, half:] = jnp.zeros((TOK, half), jnp.bfloat16)
    for u in range(Y * Z // per):
        base = u * per * WORKERS * SLICE
        block = h_ref[:, base : base + per * WORKERS * SLICE]
        for r in range(WORKERS):
            pieces = [
                block[:, (a * WORKERS + r) * SLICE : (a * WORKERS + r + 1) * SLICE] for a in range(per)
            ]
            at = (r % 2) * half + u * 128
            staged[x ^ (r // 2), :, at : at + 128] = jnp.concatenate(pieces, 1)
    for m in range(X):
        out_refs[m][...] = staged[m]


def cut_hidden(info, hidden):
    vmem = pl.BlockSpec(memory_space=pltpu.VMEM)
    part = (TOK, 2 * Y * Z * SLICE)
    return pl.pallas_call(
        cut_kernel,
        in_specs=[pl.BlockSpec(memory_space=pltpu.SMEM), vmem],
        out_specs=[vmem] * X,
        out_shape=[jax.ShapeDtypeStruct(part, jnp.bfloat16)] * X,
        scratch_shapes=[pltpu.VMEM((X,) + part, jnp.bfloat16)],
        cost_estimate=pl.CostEstimate(flops=2**34, bytes_accessed=2**24, transcendentals=0),
        name="cut_hidden",
    )(info, hidden)


def partial_kernel(info, *refs):
    h_refs, refs = refs[:X], refs[X:]
    own_refs, other_refs, out_refs = refs[:Y], refs[Y : 2 * Y], refs[2 * Y :]
    total = None
    for d in range(Y):
        for core, kv_ref in ((info[1], own_refs[d]), (1 - info[1], other_refs[d])):
            at = core * (Y * Z * SLICE) + lax.rem(info[0] + Y - d, Y) * (Z * SLICE)
            at = pl.multiple_of(at, Z * SLICE)
            rows = [h[:, pl.ds(at, Z * SLICE)] for h in h_refs]
            term = mm(jnp.concatenate(rows, 0), kv_ref[...])
            total = term if total is None else total + term
    for m in range(X):
        out_refs[m][...] = total[m * TOK : (m + 1) * TOK]


def partial_latents(info, hidden, own, other):
    vmem = pl.BlockSpec(memory_space=pltpu.VMEM)
    return pl.pallas_call(
        partial_kernel,
        in_specs=[pl.BlockSpec(memory_space=pltpu.SMEM)] + [vmem] * (X + 2 * Y),
        out_specs=[vmem] * X,
        out_shape=[jax.ShapeDtypeStruct((TOK, LAT), jnp.float32)] * X,
        compiler_params=pltpu.CompilerParams(vmem_limit_bytes=24 * 2**20),
        name="partial_latents",
    )(info, *hidden, *own, *other)


def finish_kernel(info, a_ref, b_ref, c_ref, d_ref, gain_ref, cos_ref, sin_ref, out_ref):
    latent = (a_ref[...] + b_ref[...]) + (c_ref[...] + d_ref[...])
    compressed = latent[:, :VAL]
    mean_square = jnp.mean(compressed * compressed, axis=1, keepdims=True)
    normed = compressed * lax.rsqrt(mean_square + norm_eps) * gain_ref[...]
    half = (LAT - VAL) // 2
    first, second = latent[:, VAL : VAL + half], latent[:, VAL + half :]
    cosine, sine = cos_ref[...], sin_ref[...]
    lane = lax.broadcasted_iota(jnp.int32, (TOK, AUG - LAT), 1)
    origin = jnp.where(lane == info[0], 1.0, 0.0)
    keys = jnp.concatenate(
        [normed, first * cosine - second * sine, second * cosine + first * sine, origin], 1
    ).astype(jnp.bfloat16)
    for z in range(Z):
        out_ref[z] = keys


def finish_keys(info, parts, gain, cosine, sine):
    vmem = pl.BlockSpec(memory_space=pltpu.VMEM)
    return pl.pallas_call(
        finish_kernel,
        in_specs=[pl.BlockSpec(memory_space=pltpu.SMEM)] + [vmem] * 7,
        out_specs=vmem,
        out_shape=jax.ShapeDtypeStruct((Z, TOK, AUG), jnp.bfloat16),
        name="finish_keys",
    )(info, *parts, gain, cosine, sine)


def lanes(x, n):
    return jnp.concatenate([x] * n, 1) if n > 1 else x


def attend_kernel(sub, blocks, causal, carry, final, info, *refs):
    q_ref, refs = refs[0], refs[1:]
    if carry:
        acc_ref, peak_ref, total_ref = refs[:3]
        refs = refs[3:]
    k_refs, outs = refs[:blocks], refs[blocks:]
    step = pl.program_id(0)
    subs = q_ref.shape[0] // sub
    tokens = sub // HEADS

    lane = lax.broadcasted_iota(jnp.int32, (sub, AUG - LAT), 1)
    out_of_reach = (lane > info[0]) & (lane < PAGE_LANE - LAT) | (
        (lane >= PAGE_LANE - LAT + info[1]) & (lane < PAGE_LANE - LAT + 8)
    )
    marks = jnp.where(out_of_reach, masked, 0.0).astype(jnp.bfloat16)

    def product(s):
        rows = jnp.concatenate([q_ref[s * sub : (s + 1) * sub, :], marks], 1)
        return [
            lax.dot_general(rows, k[...], (((1,), (1,)), ((), ())), preferred_element_type=jnp.float32)
            for k in k_refs
        ]

    ahead = product(0)
    for s in range(subs):
        scores = ahead
        if s + 1 < subs:
            ahead = product(s + 1)
        at = slice(s * sub, (s + 1) * sub)
        if causal:
            size = k_refs[0].shape[0]
            key = lax.broadcasted_iota(jnp.int32, (tokens, 1, size), 2)
            token = lax.broadcasted_iota(jnp.int32, (tokens, 1, size), 0)
            token = token + lax.rem(info[0], Z) * TOK + (step * subs + s) * tokens
            bias = jnp.where(key <= token, 0.0, masked)
            scores[0] = (scores[0].reshape(tokens, HEADS, size) + bias).reshape(sub, size)
        peak = None
        for score in scores:
            for j in range(0, score.shape[1], 128):
                part = score[:, j : j + 128]
                peak = part if peak is None else jnp.maximum(peak, part)
        peak = jnp.broadcast_to(jnp.max(peak, axis=1, keepdims=True), (sub, 128))
        if carry:
            peak = jnp.maximum(peak, peak_ref[at, :])
        shift = peak * exp2_scale
        total, accum = None, None
        for score, k in zip(scores, k_refs):
            count = score.shape[1] // 128
            weights = jnp.exp2(score * exp2_scale - lanes(shift, count))
            for j in range(count):
                part = weights[:, j * 128 : (j + 1) * 128]
                total = part if total is None else total + part
            term = mm(weights.astype(jnp.bfloat16), k[:, :VAL])
            accum = term if accum is None else accum + term
        if carry:
            factor = jnp.exp2(peak_ref[at, :] * exp2_scale - shift)
            total = total + total_ref[at, :] * factor
            accum = accum + acc_ref[at, :] * lanes(factor, VAL // 128)
        if final:
            outs[0][at, :] = (accum / jnp.sum(total, axis=1, keepdims=True)).astype(jnp.bfloat16)
        else:
            outs[0][at, :] = accum
            outs[1][at, :] = peak
            outs[2][at, :] = total


def attend(info, queries, carry, keys, causal, final, tile=512, sub=256):
    rows = queries.shape[0]
    row = lambda width: pl.BlockSpec((tile, width), lambda i, s: (i, 0))
    whole = lambda a: pl.BlockSpec(a.shape, lambda i, s: (0, 0))
    carry = [] if carry is None else list(carry)
    carry = [pltpu.with_memory_space_constraint(a, pltpu.VMEM) for a in carry]
    total = sum(k.shape[0] for k in keys)
    state = (VAL, 128, 128)
    if final:
        shapes = [jax.ShapeDtypeStruct((rows, VAL), jnp.bfloat16)]
        out_specs = [row(VAL)]
    else:
        shapes = [pltpu.VMEM((rows, width), jnp.float32) for width in state]
        out_specs = [row(width) for width in state]
    return pl.pallas_call(
        functools.partial(attend_kernel, sub, len(keys), causal, bool(carry), final),
        grid_spec=pltpu.PrefetchScalarGridSpec(
            num_scalar_prefetch=1,
            grid=(rows // tile,),
            in_specs=[row(LAT)]
            + [row(width) for width in state][: len(carry)]
            + [whole(k) for k in keys],
            out_specs=out_specs,
        ),
        out_shape=shapes,
        compiler_params=pltpu.CompilerParams(vmem_limit_bytes=20 * 2**20),
        cost_estimate=pl.CostEstimate(
            flops=2 * rows * total * (LAT + VAL),
            bytes_accessed=rows * 2048,
            transcendentals=rows * total,
        ),
        name="attend_last" if final else "attend_first",
    )(info, queries, *carry, *keys)


def shards(suffix_hidden, kv_down, kv_gain, queries, pool, hit_holder, hit_slot, hit_count):
    req = lax.axis_index("req").astype(jnp.int32)
    ctx = lax.axis_index("ctx").astype(jnp.int32)
    y, z = ctx // Z, ctx % Z
    count = lax.dynamic_index_in_dim(hit_count, req, 0, keepdims=False)

    piece = lax.dynamic_slice(
        kv_down, (jnp.minimum(req, WORKERS - 1) * SLICE, 0), (SLICE, LAT)
    )
    row = lax.all_to_all(
        jnp.broadcast_to(piece[None], (Z, SLICE, LAT)), "ctx", 0, 0, axis_index_groups=Z_GROUPS
    ).reshape(Z * SLICE, LAT)

    parts = cut_hidden((req // 2)[None], suffix_hidden[0])
    hidden = [parts[0]] + [
        lax.ppermute(parts[m], "req", [(i, i ^ (2 * m)) for i in range(REQ)]) for m in range(1, X)
    ]

    pool, row = lax.optimization_barrier((pool, row))
    own = [row] + [lax.ppermute(row, "ctx", y_shift(d)) for d in (1, 2, 3)]
    other = [lax.ppermute(o, "req", [(i, i ^ 1) for i in range(REQ)]) for o in own]

    sums = list(partial_latents(jnp.stack([y, req % 2]), hidden, own, other))
    sums = sums[:1] + [
        lax.ppermute(sums[m], "req", [(i, i ^ (2 * m)) for i in range(REQ)]) for m in range(1, X)
    ]

    half = (LAT - VAL) // 2
    steps = jnp.arange(half, dtype=jnp.float32) * (2.0 / (LAT - VAL))
    freqs = jnp.exp(-steps * jnp.log(rope_base))
    first = count * PAGE + ctx * TOK
    positions = (first + jnp.arange(TOK, dtype=jnp.int32)).astype(jnp.float32)
    angles = positions[:, None] * freqs[None, :]
    entries = jnp.arange(hit_holder.shape[1], dtype=jnp.int32)
    used = entries[None, :] < hit_count[:, None]
    earlier = (
        (hit_holder[:, :, None] == hit_holder[:, None, :])
        & used[:, None, :]
        & (entries[None, None, :] < entries[None, :, None])
    )
    rank = jnp.sum(earlier.astype(jnp.int32), axis=2)
    cap_ids = jnp.arange(CAP, dtype=jnp.int32)
    pick = (
        used[:, None, :]
        & (hit_holder[:, None, :] == req)
        & (rank[:, None, :] == cap_ids[None, :, None])
    )
    place = jnp.sum(jnp.where(pick, hit_slot[:, None, :], 0), axis=2)
    outgoing = jnp.take(pool[:, 0], place.reshape(-1), axis=0).reshape(REQ, CAP, LAT)
    incoming = lax.all_to_all(outgoing, "req", 0, 0).reshape(REQ * CAP, LAT)
    holder = lax.dynamic_index_in_dim(hit_holder, req, 0, keepdims=False)
    my_rank = lax.dynamic_index_in_dim(rank, req, 0, keepdims=False)
    cached = jnp.take(incoming, holder * CAP + jnp.minimum(my_rank, CAP - 1), axis=0)
    tags = jnp.broadcast_to(
        jnp.eye(8, AUG - LAT, PAGE_LANE - LAT, dtype=cached.dtype), (8, AUG - LAT)
    )
    cached = jnp.concatenate([cached, tags], 1)
    cached, sums[0] = lax.optimization_barrier((cached, sums[0]))
    cached = lax.all_to_all(
        jnp.broadcast_to(cached[None], (Y * Z,) + cached.shape), "ctx", 0, 0
    ).reshape(-1, AUG)

    fresh = finish_keys(ctx[None], sums, kv_gain[None], jnp.cos(angles), jnp.sin(angles))
    fresh, cached = lax.optimization_barrier((fresh, cached))
    near = lax.all_to_all(fresh, "ctx", 0, 0, axis_index_groups=Z_GROUPS).reshape(-1, AUG)

    far = [lax.ppermute(near, "ctx", y_shift(d)) for d in (1, 3)]

    info = jnp.stack([ctx, count]).astype(jnp.int32)
    rows = queries[0].reshape(-1, LAT)
    carry = attend(info, rows, None, [near, cached], True, False)
    far, near = lax.optimization_barrier((far, near))
    last = lax.ppermute(near, "ctx", y_shift(2))
    carry = attend(info, rows, carry, far, False, False)
    (out,) = attend(info, rows, carry, [last], False, True)
    return out.reshape(1, TOK, HEADS, VAL)


def solution(mesh):
    in_specs = (
        P("req", "ctx", None),
        P("ctx", None),
        P(),
        P("req", "ctx", None, None),
        P("req", "ctx", None),
        P(),
        P(),
        P(),
    )
    out_specs = P("req", "ctx", None, None)
    return jax.shard_map(shards, mesh=mesh, in_specs=in_specs, out_specs=out_specs, check_vma=False)
```

```python
import functools
import math

import jax
import jax.numpy as jnp
from jax import lax
from jax.experimental import pallas as pl
from jax.experimental.pallas import tpu as pltpu
from jax.sharding import PartitionSpec as P

PAGE = 32
CAP = 2
score_scale = 192.0 ** (-0.5)
rope_base = 10000.0
norm_eps = 1e-06
exp2_scale = score_scale * math.log2(math.e)
masked = -1e30

REQ, X, Y, Z = 8, 4, 4, 8
SLICE = 32
WORKERS = 7
TOK = 64
HEADS = 64
LAT = 576
VAL = 512
AUG = 640
DEVICE_LANE, PAGE_LANE = LAT, LAT + Y * Z

Z_GROUPS = [[y * Z + z for z in range(Z)] for y in range(Y)]


def y_shift(d):
    return [(i, (i + Z * d) % (Y * Z)) for i in range(Y * Z)]


def mm(a, b):
    return jnp.dot(a, b, preferred_element_type=jnp.float32)


def cut_kernel(info, h_ref, *refs):
    out_refs, staged = refs[:X], refs[X]
    x = info[0]
    per = 4
    half = Y * Z * SLICE
    staged[x ^ (X - 1), :, half:] = jnp.zeros((TOK, half), jnp.bfloat16)
    for u in range(Y * Z // per):
        base = u * per * WORKERS * SLICE
        block = h_ref[:, base : base + per * WORKERS * SLICE]
        for r in range(WORKERS):
            pieces = [
                block[:, (a * WORKERS + r) * SLICE : (a * WORKERS + r + 1) * SLICE] for a in range(per)
            ]
            at = (r % 2) * half + u * 128
            staged[x ^ (r // 2), :, at : at + 128] = jnp.concatenate(pieces, 1)
    for m in range(X):
        out_refs[m][...] = staged[m]


def cut_hidden(info, hidden):
    vmem = pl.BlockSpec(memory_space=pltpu.VMEM)
    part = (TOK, 2 * Y * Z * SLICE)
    return pl.pallas_call(
        cut_kernel,
        in_specs=[pl.BlockSpec(memory_space=pltpu.SMEM), vmem],
        out_specs=[vmem] * X,
        out_shape=[pltpu.VMEM(part, jnp.bfloat16)] + [jax.ShapeDtypeStruct(part, jnp.bfloat16)] * (X - 1),
        scratch_shapes=[pltpu.VMEM((X,) + part, jnp.bfloat16)],
        cost_estimate=pl.CostEstimate(flops=2**34, bytes_accessed=2**24, transcendentals=0),
        name="cut_hidden",
    )(info, hidden)


def partial_kernel(info, *refs):
    h_refs, refs = refs[:X], refs[X:]
    own_refs, other_refs, out_refs = refs[:Y], refs[Y : 2 * Y], refs[2 * Y :]
    total = None
    for d in range(Y):
        for core, kv_ref in ((info[1], own_refs[d]), (1 - info[1], other_refs[d])):
            at = core * (Y * Z * SLICE) + lax.rem(info[0] + Y - d, Y) * (Z * SLICE)
            at = pl.multiple_of(at, Z * SLICE)
            rows = [h[:, pl.ds(at, Z * SLICE)] for h in h_refs]
            term = mm(jnp.concatenate(rows, 0), kv_ref[...])
            total = term if total is None else total + term
    for m in range(X):
        out_refs[m][...] = total[m * TOK : (m + 1) * TOK]


def partial_latents(info, hidden, own, other):
    hidden = [pltpu.with_memory_space_constraint(h, pltpu.VMEM) for h in hidden]
    vmem = pl.BlockSpec(memory_space=pltpu.VMEM)
    return pl.pallas_call(
        partial_kernel,
        in_specs=[pl.BlockSpec(memory_space=pltpu.SMEM)] + [vmem] * (X + 2 * Y),
        out_specs=[vmem] * X,
        out_shape=[pltpu.VMEM((TOK, LAT), jnp.float32)]
        + [jax.ShapeDtypeStruct((TOK, LAT), jnp.float32)] * (X - 1),
        compiler_params=pltpu.CompilerParams(vmem_limit_bytes=24 * 2**20),
        name="partial_latents",
    )(info, *hidden, *own, *other)


def finish_kernel(info, a_ref, b_ref, c_ref, d_ref, gain_ref, cos_ref, sin_ref, out_ref):
    latent = (a_ref[...] + b_ref[...]) + (c_ref[...] + d_ref[...])
    compressed = latent[:, :VAL]
    mean_square = jnp.mean(compressed * compressed, axis=1, keepdims=True)
    normed = compressed * lax.rsqrt(mean_square + norm_eps) * gain_ref[...]
    half = (LAT - VAL) // 2
    first, second = latent[:, VAL : VAL + half], latent[:, VAL + half :]
    cosine, sine = cos_ref[...], sin_ref[...]
    lane = lax.broadcasted_iota(jnp.int32, (TOK, AUG - LAT), 1)
    origin = jnp.where(lane == info[0], 1.0, 0.0)
    keys = jnp.concatenate(
        [normed, first * cosine - second * sine, second * cosine + first * sine, origin], 1
    ).astype(jnp.bfloat16)
    for z in range(Z):
        out_ref[z] = keys


def finish_keys(info, parts, gain, cosine, sine):
    parts = [pltpu.with_memory_space_constraint(p, pltpu.VMEM) for p in parts]
    vmem = pl.BlockSpec(memory_space=pltpu.VMEM)
    return pl.pallas_call(
        finish_kernel,
        in_specs=[pl.BlockSpec(memory_space=pltpu.SMEM)] + [vmem] * 7,
        out_specs=vmem,
        out_shape=jax.ShapeDtypeStruct((Z, TOK, AUG), jnp.bfloat16),
        name="finish_keys",
    )(info, *parts, gain, cosine, sine)


def lanes(x, n):
    return jnp.concatenate([x] * n, 1) if n > 1 else x


def attend_kernel(sub, blocks, causal, carry, final, info, *refs):
    q_ref, refs = refs[0], refs[1:]
    if carry:
        acc_ref, peak_ref, total_ref = refs[:3]
        refs = refs[3:]
    k_refs, outs = refs[:blocks], refs[blocks:]
    step = pl.program_id(0)
    subs = q_ref.shape[0] // sub
    tokens = sub // HEADS

    lane = lax.broadcasted_iota(jnp.int32, (sub, AUG - LAT), 1)
    out_of_reach = (lane > info[0]) & (lane < PAGE_LANE - LAT) | (
        (lane >= PAGE_LANE - LAT + info[1]) & (lane < PAGE_LANE - LAT + 8)
    )
    marks = jnp.where(out_of_reach, masked, 0.0).astype(jnp.bfloat16)

    def product(s):
        rows = jnp.concatenate([q_ref[s * sub : (s + 1) * sub, :], marks], 1)
        return [
            lax.dot_general(rows, k[...], (((1,), (1,)), ((), ())), preferred_element_type=jnp.float32)
            for k in k_refs
        ]

    ahead = product(0)
    for s in range(subs):
        scores = ahead
        if s + 1 < subs:
            ahead = product(s + 1)
        at = slice(s * sub, (s + 1) * sub)
        if causal:
            size = k_refs[0].shape[0]
            key = lax.broadcasted_iota(jnp.int32, (tokens, 1, size), 2)
            token = lax.broadcasted_iota(jnp.int32, (tokens, 1, size), 0)
            token = token + lax.rem(info[0], Z) * TOK + (step * subs + s) * tokens
            bias = jnp.where(key <= token, 0.0, masked)
            scores[0] = (scores[0].reshape(tokens, HEADS, size) + bias).reshape(sub, size)
        peak = None
        for score in scores:
            for j in range(0, score.shape[1], 128):
                part = score[:, j : j + 128]
                peak = part if peak is None else jnp.maximum(peak, part)
        peak = jnp.broadcast_to(jnp.max(peak, axis=1, keepdims=True), (sub, 128))
        if carry:
            peak = jnp.maximum(peak, peak_ref[at, :])
        shift = peak * exp2_scale
        total, accum = None, None
        for score, k in zip(scores, k_refs):
            count = score.shape[1] // 128
            weights = jnp.exp2(score * exp2_scale - lanes(shift, count))
            for j in range(count):
                part = weights[:, j * 128 : (j + 1) * 128]
                total = part if total is None else total + part
            term = mm(weights.astype(jnp.bfloat16), k[:, :VAL])
            accum = term if accum is None else accum + term
        if carry:
            factor = jnp.exp2(peak_ref[at, :] * exp2_scale - shift)
            total = total + total_ref[at, :] * factor
            accum = accum + acc_ref[at, :] * lanes(factor, VAL // 128)
        if final:
            outs[0][at, :] = (accum / jnp.sum(total, axis=1, keepdims=True)).astype(jnp.bfloat16)
        else:
            outs[0][at, :] = accum
            outs[1][at, :] = peak
            outs[2][at, :] = total


def attend(info, queries, carry, keys, causal, final, tile=512, sub=256):
    rows = queries.shape[0]
    row = lambda width: pl.BlockSpec((tile, width), lambda i, s: (i, 0))
    whole = lambda a: pl.BlockSpec(a.shape, lambda i, s: (0, 0))
    carry = [] if carry is None else list(carry)
    carry = [pltpu.with_memory_space_constraint(a, pltpu.VMEM) for a in carry]
    total = sum(k.shape[0] for k in keys)
    state = (VAL, 128, 128)
    if final:
        shapes = [jax.ShapeDtypeStruct((rows, VAL), jnp.bfloat16)]
        out_specs = [row(VAL)]
    else:
        shapes = [pltpu.VMEM((rows, width), jnp.float32) for width in state]
        out_specs = [row(width) for width in state]
    return pl.pallas_call(
        functools.partial(attend_kernel, sub, len(keys), causal, bool(carry), final),
        grid_spec=pltpu.PrefetchScalarGridSpec(
            num_scalar_prefetch=1,
            grid=(rows // tile,),
            in_specs=[row(LAT)]
            + [row(width) for width in state][: len(carry)]
            + [whole(k) for k in keys],
            out_specs=out_specs,
        ),
        out_shape=shapes,
        compiler_params=pltpu.CompilerParams(vmem_limit_bytes=20 * 2**20),
        cost_estimate=pl.CostEstimate(
            flops=2 * rows * total * (LAT + VAL),
            bytes_accessed=rows * 2048,
            transcendentals=rows * total,
        ),
        name="attend_last" if final else "attend_first",
    )(info, queries, *carry, *keys)


def shards(suffix_hidden, kv_down, kv_gain, queries, pool, hit_holder, hit_slot, hit_count):
    req = lax.axis_index("req").astype(jnp.int32)
    ctx = lax.axis_index("ctx").astype(jnp.int32)
    y, z = ctx // Z, ctx % Z
    count = lax.dynamic_index_in_dim(hit_count, req, 0, keepdims=False)

    piece = lax.dynamic_slice(
        kv_down, (jnp.minimum(req, WORKERS - 1) * SLICE, 0), (SLICE, LAT)
    )
    row = lax.all_to_all(
        jnp.broadcast_to(piece[None], (Z, SLICE, LAT)), "ctx", 0, 0, axis_index_groups=Z_GROUPS
    ).reshape(Z * SLICE, LAT)

    parts = list(cut_hidden((req // 2)[None], suffix_hidden[0]))
    hidden = parts[:1] + [
        lax.ppermute(parts[m], "req", [(i, i ^ (2 * m)) for i in range(REQ)]) for m in range(1, X)
    ]

    half = (LAT - VAL) // 2
    steps = jnp.arange(half, dtype=jnp.float32) * (2.0 / (LAT - VAL))
    freqs = jnp.exp(-steps * jnp.log(rope_base))
    first = count * PAGE + ctx * TOK
    positions = (first + jnp.arange(TOK, dtype=jnp.int32)).astype(jnp.float32)
    angles = positions[:, None] * freqs[None, :]
    cosine, sine = jnp.cos(angles), jnp.sin(angles)
    info = jnp.stack([ctx, count]).astype(jnp.int32)
    info, cosine, sine, hidden[0] = lax.optimization_barrier((info, cosine, sine, hidden[0]))

    pool, row = lax.optimization_barrier((pool, row))
    own = [row] + [lax.ppermute(row, "ctx", y_shift(d)) for d in (1, 2, 3)]
    other = [lax.ppermute(o, "req", [(i, i ^ 1) for i in range(REQ)]) for o in own]

    sums = list(partial_latents(jnp.stack([y, req % 2]), hidden, own, other))
    sums = sums[:1] + [
        lax.ppermute(sums[m], "req", [(i, i ^ (2 * m)) for i in range(REQ)]) for m in range(1, X)
    ]

    entries = jnp.arange(hit_holder.shape[1], dtype=jnp.int32)
    used = entries[None, :] < hit_count[:, None]
    earlier = (
        (hit_holder[:, :, None] == hit_holder[:, None, :])
        & used[:, None, :]
        & (entries[None, None, :] < entries[None, :, None])
    )
    rank = jnp.sum(earlier.astype(jnp.int32), axis=2)
    cap_ids = jnp.arange(CAP, dtype=jnp.int32)
    pick = (
        used[:, None, :]
        & (hit_holder[:, None, :] == req)
        & (rank[:, None, :] == cap_ids[None, :, None])
    )
    place = jnp.sum(jnp.where(pick, hit_slot[:, None, :], 0), axis=2)
    outgoing = jnp.take(pool[:, 0], place.reshape(-1), axis=0).reshape(REQ, CAP, LAT)
    incoming = lax.all_to_all(outgoing, "req", 0, 0).reshape(REQ * CAP, LAT)
    holder = lax.dynamic_index_in_dim(hit_holder, req, 0, keepdims=False)
    my_rank = lax.dynamic_index_in_dim(rank, req, 0, keepdims=False)
    cached = jnp.take(incoming, holder * CAP + jnp.minimum(my_rank, CAP - 1), axis=0)
    tags = jnp.broadcast_to(
        jnp.eye(8, AUG - LAT, PAGE_LANE - LAT, dtype=cached.dtype), (8, AUG - LAT)
    )
    cached = jnp.concatenate([cached, tags], 1)
    cached, sums[0] = lax.optimization_barrier((cached, sums[0]))
    cached = lax.all_to_all(
        jnp.broadcast_to(cached[None], (Y * Z,) + cached.shape), "ctx", 0, 0
    ).reshape(-1, AUG)

    fresh = finish_keys(info, sums, kv_gain[None], cosine, sine)
    fresh, cached = lax.optimization_barrier((fresh, cached))
    near = lax.all_to_all(fresh, "ctx", 0, 0, axis_index_groups=Z_GROUPS).reshape(-1, AUG)

    far = [lax.ppermute(near, "ctx", y_shift(d)) for d in (1, 3)]

    rows = queries[0].reshape(-1, LAT)
    carry = attend(info, rows, None, [near, cached], True, False)
    far, near = lax.optimization_barrier((far, near))
    last = lax.ppermute(near, "ctx", y_shift(2))
    carry = attend(info, rows, carry, far, False, False)
    (out,) = attend(info, rows, carry, [last], False, True)
    return out.reshape(1, TOK, HEADS, VAL)


def solution(mesh):
    in_specs = (
        P("req", "ctx", None),
        P("ctx", None),
        P(),
        P("req", "ctx", None, None),
        P("req", "ctx", None),
        P(),
        P(),
        P(),
    )
    out_specs = P("req", "ctx", None, None)
    return jax.shard_map(shards, mesh=mesh, in_specs=in_specs, out_specs=out_specs, check_vma=False)
```

```python
import functools
import math

import jax
import jax.numpy as jnp
from jax import lax
from jax.experimental import pallas as pl
from jax.experimental.pallas import tpu as pltpu
from jax.sharding import PartitionSpec as P

PAGE = 32
CAP = 2
score_scale = 192.0 ** (-0.5)
rope_base = 10000.0
norm_eps = 1e-06
exp2_scale = score_scale * math.log2(math.e)
masked = -1e30

REQ, X, Y, Z = 8, 4, 4, 8
SLICE = 32
WORKERS = 7
TOK = 64
HEADS = 64
LAT = 576
VAL = 512
AUG = 640
DEVICE_LANE, PAGE_LANE = LAT, LAT + Y * Z

Z_GROUPS = [[y * Z + z for z in range(Z)] for y in range(Y)]


def y_shift(d):
    return [(i, (i + Z * d) % (Y * Z)) for i in range(Y * Z)]


def mm(a, b):
    return jnp.dot(a, b, preferred_element_type=jnp.float32)


def cut_kernel(info, h_ref, *refs):
    out_refs, staged = refs[:X], refs[X]
    x = info[0]
    per = 4
    half = Y * Z * SLICE
    staged[x ^ (X - 1), :, half:] = jnp.zeros((TOK, half), jnp.bfloat16)
    for u in range(Y * Z // per):
        base = u * per * WORKERS * SLICE
        block = h_ref[:, base : base + per * WORKERS * SLICE]
        for r in range(WORKERS):
            pieces = [
                block[:, (a * WORKERS + r) * SLICE : (a * WORKERS + r + 1) * SLICE] for a in range(per)
            ]
            at = (r % 2) * half + u * 128
            staged[x ^ (r // 2), :, at : at + 128] = jnp.concatenate(pieces, 1)
    for m in range(X):
        out_refs[m][...] = staged[m]


def cut_hidden(info, hidden):
    vmem = pl.BlockSpec(memory_space=pltpu.VMEM)
    part = (TOK, 2 * Y * Z * SLICE)
    return pl.pallas_call(
        cut_kernel,
        in_specs=[pl.BlockSpec(memory_space=pltpu.SMEM), vmem],
        out_specs=[vmem] * X,
        out_shape=[pltpu.VMEM(part, jnp.bfloat16)] + [jax.ShapeDtypeStruct(part, jnp.bfloat16)] * (X - 1),
        scratch_shapes=[pltpu.VMEM((X,) + part, jnp.bfloat16)],
        cost_estimate=pl.CostEstimate(flops=2**34, bytes_accessed=2**24, transcendentals=0),
        name="cut_hidden",
    )(info, hidden)


def partial_kernel(info, *refs):
    h_refs, refs = refs[:X], refs[X:]
    own_refs, other_refs, out_refs = refs[:Y], refs[Y : 2 * Y], refs[2 * Y :]
    total = None
    for d in range(Y):
        for core, kv_ref in ((info[1], own_refs[d]), (1 - info[1], other_refs[d])):
            at = core * (Y * Z * SLICE) + lax.rem(info[0] + Y - d, Y) * (Z * SLICE)
            at = pl.multiple_of(at, Z * SLICE)
            rows = [h[:, pl.ds(at, Z * SLICE)] for h in h_refs]
            term = mm(jnp.concatenate(rows, 0), kv_ref[...])
            total = term if total is None else total + term
    for m in range(X):
        out_refs[m][...] = total[m * TOK : (m + 1) * TOK]


def partial_latents(info, hidden, own, other):
    hidden = [pltpu.with_memory_space_constraint(h, pltpu.VMEM) for h in hidden]
    vmem = pl.BlockSpec(memory_space=pltpu.VMEM)
    return pl.pallas_call(
        partial_kernel,
        in_specs=[pl.BlockSpec(memory_space=pltpu.SMEM)] + [vmem] * (X + 2 * Y),
        out_specs=[vmem] * X,
        out_shape=[pltpu.VMEM((TOK, LAT), jnp.float32)]
        + [jax.ShapeDtypeStruct((TOK, LAT), jnp.float32)] * (X - 1),
        compiler_params=pltpu.CompilerParams(vmem_limit_bytes=24 * 2**20),
        name="partial_latents",
    )(info, *hidden, *own, *other)


def finish_kernel(info, a_ref, b_ref, c_ref, d_ref, gain_ref, cos_ref, sin_ref, out_ref):
    latent = (a_ref[...] + b_ref[...]) + (c_ref[...] + d_ref[...])
    compressed = latent[:, :VAL]
    mean_square = jnp.mean(compressed * compressed, axis=1, keepdims=True)
    normed = compressed * lax.rsqrt(mean_square + norm_eps) * gain_ref[...]
    half = (LAT - VAL) // 2
    first, second = latent[:, VAL : VAL + half], latent[:, VAL + half :]
    cosine, sine = cos_ref[...], sin_ref[...]
    lane = lax.broadcasted_iota(jnp.int32, (TOK, AUG - LAT), 1)
    origin = jnp.where(lane == info[0], 1.0, 0.0)
    keys = jnp.concatenate(
        [normed, first * cosine - second * sine, second * cosine + first * sine, origin], 1
    ).astype(jnp.bfloat16)
    for z in range(Z):
        out_ref[z] = keys


def finish_keys(info, parts, gain, cosine, sine):
    parts = [pltpu.with_memory_space_constraint(p, pltpu.VMEM) for p in parts]
    vmem = pl.BlockSpec(memory_space=pltpu.VMEM)
    return pl.pallas_call(
        finish_kernel,
        in_specs=[pl.BlockSpec(memory_space=pltpu.SMEM)] + [vmem] * 7,
        out_specs=vmem,
        out_shape=jax.ShapeDtypeStruct((Z, TOK, AUG), jnp.bfloat16),
        name="finish_keys",
    )(info, *parts, gain, cosine, sine)


def lanes(x, n):
    return jnp.concatenate([x] * n, 1) if n > 1 else x


def attend_kernel(sub, blocks, causal, carry, final, info, *refs):
    q_ref, refs = refs[0], refs[1:]
    if carry:
        acc_ref, peak_ref, total_ref = refs[:3]
        refs = refs[3:]
    k_refs, outs = refs[:blocks], refs[blocks:]
    step = pl.program_id(0)
    subs = q_ref.shape[0] // sub
    tokens = sub // HEADS

    lane = lax.broadcasted_iota(jnp.int32, (sub, AUG - LAT), 1)
    out_of_reach = (lane > info[0]) & (lane < PAGE_LANE - LAT) | (
        (lane >= PAGE_LANE - LAT + info[1]) & (lane < PAGE_LANE - LAT + 8)
    )
    marks = jnp.where(out_of_reach, masked, 0.0).astype(jnp.bfloat16)

    def product(s):
        rows = jnp.concatenate([q_ref[s * sub : (s + 1) * sub, :], marks], 1)
        return [
            lax.dot_general(rows, k[...], (((1,), (1,)), ((), ())), preferred_element_type=jnp.float32)
            for k in k_refs
        ]

    ahead = product(0)
    for s in range(subs):
        scores = ahead
        if s + 1 < subs:
            ahead = product(s + 1)
        at = slice(s * sub, (s + 1) * sub)
        if causal:
            size = k_refs[0].shape[0]
            key = lax.broadcasted_iota(jnp.int32, (tokens, 1, size), 2)
            token = lax.broadcasted_iota(jnp.int32, (tokens, 1, size), 0)
            token = token + lax.rem(info[0], Z) * TOK + (step * subs + s) * tokens
            bias = jnp.where(key <= token, 0.0, masked)
            scores[0] = (scores[0].reshape(tokens, HEADS, size) + bias).reshape(sub, size)
        peak = None
        for score in scores:
            for j in range(0, score.shape[1], 128):
                part = score[:, j : j + 128]
                peak = part if peak is None else jnp.maximum(peak, part)
        peak = jnp.broadcast_to(jnp.max(peak, axis=1, keepdims=True), (sub, 128))
        if carry:
            peak = jnp.maximum(peak, peak_ref[at, :])
        shift = peak * exp2_scale
        total, accum = None, None
        for score, k in zip(scores, k_refs):
            count = score.shape[1] // 128
            weights = jnp.exp2(score * exp2_scale - lanes(shift, count))
            for j in range(count):
                part = weights[:, j * 128 : (j + 1) * 128]
                total = part if total is None else total + part
            term = mm(weights.astype(jnp.bfloat16), k[:, :VAL])
            accum = term if accum is None else accum + term
        if carry:
            factor = jnp.exp2(peak_ref[at, :] * exp2_scale - shift)
            total = total + total_ref[at, :] * factor
            accum = accum + acc_ref[at, :] * lanes(factor, VAL // 128)
        if final:
            outs[0][at, :] = (accum / jnp.sum(total, axis=1, keepdims=True)).astype(jnp.bfloat16)
        else:
            outs[0][at, :] = accum
            outs[1][at, :] = peak
            outs[2][at, :] = total


def attend(info, queries, carry, keys, causal, final, tile=512, sub=256):
    rows = queries.shape[0]
    row = lambda width: pl.BlockSpec((tile, width), lambda i, s: (i, 0))
    whole = lambda a: pl.BlockSpec(a.shape, lambda i, s: (0, 0))
    carry = [] if carry is None else list(carry)
    carry = [pltpu.with_memory_space_constraint(a, pltpu.VMEM) for a in carry]
    total = sum(k.shape[0] for k in keys)
    state = (VAL, 128, 128)
    if final:
        shapes = [jax.ShapeDtypeStruct((rows, VAL), jnp.bfloat16)]
        out_specs = [row(VAL)]
    else:
        shapes = [pltpu.VMEM((rows, width), jnp.float32) for width in state]
        out_specs = [row(width) for width in state]
    return pl.pallas_call(
        functools.partial(attend_kernel, sub, len(keys), causal, bool(carry), final),
        grid_spec=pltpu.PrefetchScalarGridSpec(
            num_scalar_prefetch=1,
            grid=(rows // tile,),
            in_specs=[row(LAT)]
            + [row(width) for width in state][: len(carry)]
            + [whole(k) for k in keys],
            out_specs=out_specs,
        ),
        out_shape=shapes,
        compiler_params=pltpu.CompilerParams(vmem_limit_bytes=20 * 2**20),
        cost_estimate=pl.CostEstimate(
            flops=2 * rows * total * (LAT + VAL),
            bytes_accessed=rows * 2048,
            transcendentals=rows * total,
        ),
        name="attend_last" if final else "attend_first",
    )(info, queries, *carry, *keys)


def shards(suffix_hidden, kv_down, kv_gain, queries, pool, hit_holder, hit_slot, hit_count):
    req = lax.axis_index("req").astype(jnp.int32)
    ctx = lax.axis_index("ctx").astype(jnp.int32)
    y, z = ctx // Z, ctx % Z
    count = lax.dynamic_index_in_dim(hit_count, req, 0, keepdims=False)

    piece = lax.dynamic_slice(
        kv_down, (jnp.minimum(req, WORKERS - 1) * SLICE, 0), (SLICE, LAT)
    )
    row = lax.all_to_all(
        jnp.broadcast_to(piece[None], (Z, SLICE, LAT)), "ctx", 0, 0, axis_index_groups=Z_GROUPS
    ).reshape(Z * SLICE, LAT)

    parts = list(cut_hidden((req // 2)[None], suffix_hidden[0]))
    hidden = parts[:1] + [
        lax.ppermute(parts[m], "req", [(i, i ^ (2 * m)) for i in range(REQ)]) for m in range(1, X)
    ]

    half = (LAT - VAL) // 2
    steps = jnp.arange(half, dtype=jnp.float32) * (2.0 / (LAT - VAL))
    freqs = jnp.exp(-steps * jnp.log(rope_base))
    first = count * PAGE + ctx * TOK
    positions = (first + jnp.arange(TOK, dtype=jnp.int32)).astype(jnp.float32)
    angles = positions[:, None] * freqs[None, :]
    cosine, sine = jnp.cos(angles), jnp.sin(angles)
    info = jnp.stack([ctx, count]).astype(jnp.int32)
    info, cosine, sine, hidden[0] = lax.optimization_barrier((info, cosine, sine, hidden[0]))

    pool, row = lax.optimization_barrier((pool, row))
    pool = lax.optimization_barrier((pool, hidden[3]))[0]
    own = [row] + [lax.ppermute(row, "ctx", y_shift(d)) for d in (1, 2, 3)]
    other = [lax.ppermute(o, "req", [(i, i ^ 1) for i in range(REQ)]) for o in own]

    sums = list(partial_latents(jnp.stack([y, req % 2]), hidden, own, other))
    sums = sums[:1] + [
        lax.ppermute(sums[m], "req", [(i, i ^ (2 * m)) for i in range(REQ)]) for m in range(1, X)
    ]

    entries = jnp.arange(hit_holder.shape[1], dtype=jnp.int32)
    used = entries[None, :] < hit_count[:, None]
    earlier = (
        (hit_holder[:, :, None] == hit_holder[:, None, :])
        & used[:, None, :]
        & (entries[None, None, :] < entries[None, :, None])
    )
    rank = jnp.sum(earlier.astype(jnp.int32), axis=2)
    cap_ids = jnp.arange(CAP, dtype=jnp.int32)
    pick = (
        used[:, None, :]
        & (hit_holder[:, None, :] == req)
        & (rank[:, None, :] == cap_ids[None, :, None])
    )
    place = jnp.sum(jnp.where(pick, hit_slot[:, None, :], 0), axis=2)
    outgoing = jnp.take(pool[:, 0], place.reshape(-1), axis=0).reshape(REQ, CAP, LAT)
    incoming = lax.all_to_all(outgoing, "req", 0, 0).reshape(REQ * CAP, LAT)
    holder = lax.dynamic_index_in_dim(hit_holder, req, 0, keepdims=False)
    my_rank = lax.dynamic_index_in_dim(rank, req, 0, keepdims=False)
    cached = jnp.take(incoming, holder * CAP + jnp.minimum(my_rank, CAP - 1), axis=0)
    tags = jnp.broadcast_to(
        jnp.eye(8, AUG - LAT, PAGE_LANE - LAT, dtype=cached.dtype), (8, AUG - LAT)
    )
    cached = jnp.concatenate([cached, tags], 1)
    cached, sums[0] = lax.optimization_barrier((cached, sums[0]))
    cached = lax.all_to_all(
        jnp.broadcast_to(cached[None], (Y * Z,) + cached.shape), "ctx", 0, 0
    ).reshape(-1, AUG)

    fresh = finish_keys(info, sums, kv_gain[None], cosine, sine)
    fresh, cached = lax.optimization_barrier((fresh, cached))
    near = lax.all_to_all(fresh, "ctx", 0, 0, axis_index_groups=Z_GROUPS).reshape(-1, AUG)

    far = [lax.ppermute(near, "ctx", y_shift(d)) for d in (1, 3)]

    rows = queries[0].reshape(-1, LAT)
    carry = attend(info, rows, None, [near, cached], True, False)
    far, near = lax.optimization_barrier((far, near))
    last = lax.ppermute(near, "ctx", y_shift(2))
    carry = attend(info, rows, carry, far, False, False)
    (out,) = attend(info, rows, carry, [last], False, True)
    return out.reshape(1, TOK, HEADS, VAL)


def solution(mesh):
    in_specs = (
        P("req", "ctx", None),
        P("ctx", None),
        P(),
        P("req", "ctx", None, None),
        P("req", "ctx", None),
        P(),
        P(),
        P(),
    )
    out_specs = P("req", "ctx", None, None)
    return jax.shard_map(shards, mesh=mesh, in_specs=in_specs, out_specs=out_specs, check_vma=False)
```

```python
import functools
import math

import jax
import jax.numpy as jnp
from jax import lax
from jax.experimental import pallas as pl
from jax.experimental.pallas import tpu as pltpu
from jax.sharding import PartitionSpec as P

PAGE = 32
CAP = 2
score_scale = 192.0 ** (-0.5)
rope_base = 10000.0
norm_eps = 1e-06
exp2_scale = score_scale * math.log2(math.e)
masked = -1e30

REQ, X, Y, Z = 8, 4, 4, 8
SLICE = 32
WORKERS = 7
TOK = 64
HEADS = 64
LAT = 576
VAL = 512
AUG = 640
DEVICE_LANE, PAGE_LANE = LAT, LAT + Y * Z

Z_GROUPS = [[y * Z + z for z in range(Z)] for y in range(Y)]


def y_shift(d):
    return [(i, (i + Z * d) % (Y * Z)) for i in range(Y * Z)]


def mm(a, b):
    return jnp.dot(a, b, preferred_element_type=jnp.float32)


def cut_kernel(info, h_ref, *refs):
    out_refs, staged = refs[:X], refs[X]
    x = info[0]
    per = 4
    half = Y * Z * SLICE
    staged[x ^ (X - 1), :, half:] = jnp.zeros((TOK, half), jnp.bfloat16)
    for u in range(Y * Z // per):
        base = u * per * WORKERS * SLICE
        block = h_ref[:, base : base + per * WORKERS * SLICE]
        for r in range(WORKERS):
            pieces = [
                block[:, (a * WORKERS + r) * SLICE : (a * WORKERS + r + 1) * SLICE] for a in range(per)
            ]
            at = (r % 2) * half + u * 128
            staged[x ^ (r // 2), :, at : at + 128] = jnp.concatenate(pieces, 1)
    for m in range(X):
        out_refs[m][...] = staged[m]


def cut_hidden(info, hidden):
    vmem = pl.BlockSpec(memory_space=pltpu.VMEM)
    part = (TOK, 2 * Y * Z * SLICE)
    return pl.pallas_call(
        cut_kernel,
        in_specs=[pl.BlockSpec(memory_space=pltpu.SMEM), vmem],
        out_specs=[vmem] * X,
        out_shape=[pltpu.VMEM(part, jnp.bfloat16)] + [jax.ShapeDtypeStruct(part, jnp.bfloat16)] * (X - 1),
        scratch_shapes=[pltpu.VMEM((X,) + part, jnp.bfloat16)],
        cost_estimate=pl.CostEstimate(flops=2**34, bytes_accessed=2**24, transcendentals=0),
        name="cut_hidden",
    )(info, hidden)


def partial_kernel(info, *refs):
    h_refs, refs = refs[:X], refs[X:]
    own_refs, other_refs, out_refs = refs[:Y], refs[Y : 2 * Y], refs[2 * Y :]
    total = None
    for d in range(Y):
        for core, kv_ref in ((info[1], own_refs[d]), (1 - info[1], other_refs[d])):
            at = core * (Y * Z * SLICE) + lax.rem(info[0] + Y - d, Y) * (Z * SLICE)
            at = pl.multiple_of(at, Z * SLICE)
            rows = [h[:, pl.ds(at, Z * SLICE)] for h in h_refs]
            term = mm(jnp.concatenate(rows, 0), kv_ref[...])
            total = term if total is None else total + term
    for m in range(X):
        out_refs[m][...] = total[m * TOK : (m + 1) * TOK]


def partial_latents(info, hidden, own, other):
    hidden = [pltpu.with_memory_space_constraint(h, pltpu.VMEM) for h in hidden]
    vmem = pl.BlockSpec(memory_space=pltpu.VMEM)
    return pl.pallas_call(
        partial_kernel,
        in_specs=[pl.BlockSpec(memory_space=pltpu.SMEM)] + [vmem] * (X + 2 * Y),
        out_specs=[vmem] * X,
        out_shape=[pltpu.VMEM((TOK, LAT), jnp.float32)]
        + [jax.ShapeDtypeStruct((TOK, LAT), jnp.float32)] * (X - 1),
        compiler_params=pltpu.CompilerParams(vmem_limit_bytes=24 * 2**20),
        name="partial_latents",
    )(info, *hidden, *own, *other)


def finish_kernel(info, a_ref, b_ref, c_ref, d_ref, gain_ref, cos_ref, sin_ref, out_ref):
    latent = (a_ref[...] + b_ref[...]) + (c_ref[...] + d_ref[...])
    compressed = latent[:, :VAL]
    mean_square = jnp.mean(compressed * compressed, axis=1, keepdims=True)
    normed = compressed * lax.rsqrt(mean_square + norm_eps) * gain_ref[...]
    half = (LAT - VAL) // 2
    first, second = latent[:, VAL : VAL + half], latent[:, VAL + half :]
    cosine, sine = cos_ref[...], sin_ref[...]
    lane = lax.broadcasted_iota(jnp.int32, (TOK, AUG - LAT), 1)
    origin = jnp.where(lane == info[0], 1.0, 0.0)
    keys = jnp.concatenate(
        [normed, first * cosine - second * sine, second * cosine + first * sine, origin], 1
    ).astype(jnp.bfloat16)
    for z in range(Z):
        out_ref[z] = keys


def finish_keys(info, parts, gain, cosine, sine):
    parts = [pltpu.with_memory_space_constraint(p, pltpu.VMEM) for p in parts]
    vmem = pl.BlockSpec(memory_space=pltpu.VMEM)
    return pl.pallas_call(
        finish_kernel,
        in_specs=[pl.BlockSpec(memory_space=pltpu.SMEM)] + [vmem] * 7,
        out_specs=vmem,
        out_shape=jax.ShapeDtypeStruct((Z, TOK, AUG), jnp.bfloat16),
        name="finish_keys",
    )(info, *parts, gain, cosine, sine)


def lanes(x, n):
    return jnp.concatenate([x] * n, 1) if n > 1 else x


def attend_kernel(sub, blocks, causal, carry, final, info, *refs):
    q_ref, refs = refs[0], refs[1:]
    if carry:
        acc_ref, peak_ref, total_ref = refs[:3]
        refs = refs[3:]
    k_refs, outs = refs[:blocks], refs[blocks:]
    step = pl.program_id(0)
    subs = q_ref.shape[0] // sub
    tokens = sub // HEADS

    lane = lax.broadcasted_iota(jnp.int32, (sub, AUG - LAT), 1)
    out_of_reach = (lane > info[0]) & (lane < PAGE_LANE - LAT) | (
        (lane >= PAGE_LANE - LAT + info[1]) & (lane < PAGE_LANE - LAT + 8)
    )
    marks = jnp.where(out_of_reach, masked, 0.0).astype(jnp.bfloat16)

    def product(s):
        rows = jnp.concatenate([q_ref[s * sub : (s + 1) * sub, :], marks], 1)
        return [
            lax.dot_general(rows, k[...], (((1,), (1,)), ((), ())), preferred_element_type=jnp.float32)
            for k in k_refs
        ]

    ahead = product(0)
    for s in range(subs):
        scores = ahead
        if s + 1 < subs:
            ahead = product(s + 1)
        at = slice(s * sub, (s + 1) * sub)
        if causal:
            size = k_refs[0].shape[0]
            key = lax.broadcasted_iota(jnp.int32, (tokens, 1, size), 2)
            token = lax.broadcasted_iota(jnp.int32, (tokens, 1, size), 0)
            token = token + lax.rem(info[0], Z) * TOK + (step * subs + s) * tokens
            bias = jnp.where(key <= token, 0.0, masked)
            scores[0] = (scores[0].reshape(tokens, HEADS, size) + bias).reshape(sub, size)
        peak = None
        for score in scores:
            for j in range(0, score.shape[1], 128):
                part = score[:, j : j + 128]
                peak = part if peak is None else jnp.maximum(peak, part)
        peak = jnp.broadcast_to(jnp.max(peak, axis=1, keepdims=True), (sub, 128))
        if carry:
            peak = jnp.maximum(peak, peak_ref[at, :])
        shift = peak * exp2_scale
        total, accum = None, None
        for score, k in zip(scores, k_refs):
            count = score.shape[1] // 128
            weights = jnp.exp2(score * exp2_scale - lanes(shift, count))
            for j in range(count):
                part = weights[:, j * 128 : (j + 1) * 128]
                total = part if total is None else total + part
            term = mm(weights.astype(jnp.bfloat16), k[:, :VAL])
            accum = term if accum is None else accum + term
        if carry:
            factor = jnp.exp2(peak_ref[at, :] * exp2_scale - shift)
            total = total + total_ref[at, :] * factor
            accum = accum + acc_ref[at, :] * lanes(factor, VAL // 128)
        if final:
            outs[0][at, :] = (accum / jnp.sum(total, axis=1, keepdims=True)).astype(jnp.bfloat16)
        else:
            outs[0][at, :] = accum
            outs[1][at, :] = peak
            outs[2][at, :] = total


def attend(info, queries, carry, keys, causal, final, tile=512, sub=256):
    rows = queries.shape[0]
    row = lambda width: pl.BlockSpec((tile, width), lambda i, s: (i, 0))
    whole = lambda a: pl.BlockSpec(a.shape, lambda i, s: (0, 0))
    carry = [] if carry is None else list(carry)
    carry = [pltpu.with_memory_space_constraint(a, pltpu.VMEM) for a in carry]
    total = sum(k.shape[0] for k in keys)
    state = (VAL, 128, 128)
    if final:
        shapes = [jax.ShapeDtypeStruct((rows, VAL), jnp.bfloat16)]
        out_specs = [row(VAL)]
    else:
        shapes = [pltpu.VMEM((rows, width), jnp.float32) for width in state]
        out_specs = [row(width) for width in state]
    return pl.pallas_call(
        functools.partial(attend_kernel, sub, len(keys), causal, bool(carry), final),
        grid_spec=pltpu.PrefetchScalarGridSpec(
            num_scalar_prefetch=1,
            grid=(rows // tile,),
            in_specs=[row(LAT)]
            + [row(width) for width in state][: len(carry)]
            + [whole(k) for k in keys],
            out_specs=out_specs,
        ),
        out_shape=shapes,
        compiler_params=pltpu.CompilerParams(vmem_limit_bytes=20 * 2**20),
        cost_estimate=pl.CostEstimate(
            flops=2 * rows * total * (LAT + VAL),
            bytes_accessed=rows * 2048,
            transcendentals=rows * total,
        ),
        name="attend_last" if final else "attend_first",
    )(info, queries, *carry, *keys)


def shards(suffix_hidden, kv_down, kv_gain, queries, pool, hit_holder, hit_slot, hit_count):
    req = lax.axis_index("req").astype(jnp.int32)
    ctx = lax.axis_index("ctx").astype(jnp.int32)
    y, z = ctx // Z, ctx % Z
    count = lax.dynamic_index_in_dim(hit_count, req, 0, keepdims=False)

    piece = lax.dynamic_slice(
        kv_down, (jnp.minimum(req, WORKERS - 1) * SLICE, 0), (SLICE, LAT)
    )
    row = lax.all_to_all(
        jnp.broadcast_to(piece[None], (Z, SLICE, LAT)), "ctx", 0, 0, axis_index_groups=Z_GROUPS
    ).reshape(Z * SLICE, LAT)

    parts = list(cut_hidden((req // 2)[None], suffix_hidden[0]))
    hidden = parts[:1] + [
        lax.ppermute(parts[m], "req", [(i, i ^ (2 * m)) for i in range(REQ)]) for m in range(1, X)
    ]

    half = (LAT - VAL) // 2
    steps = jnp.arange(half, dtype=jnp.float32) * (2.0 / (LAT - VAL))
    freqs = jnp.exp(-steps * jnp.log(rope_base))
    first = count * PAGE + ctx * TOK
    positions = (first + jnp.arange(TOK, dtype=jnp.int32)).astype(jnp.float32)
    angles = positions[:, None] * freqs[None, :]
    cosine, sine = jnp.cos(angles), jnp.sin(angles)
    info = jnp.stack([ctx, count]).astype(jnp.int32)
    info, cosine, sine, hidden[0] = lax.optimization_barrier((info, cosine, sine, hidden[0]))

    pool, row = lax.optimization_barrier((pool, row))
    pool = lax.optimization_barrier((pool, hidden[3]))[0]
    own = [row] + [lax.ppermute(row, "ctx", y_shift(d)) for d in (1, 2, 3)]
    other = [lax.ppermute(o, "req", [(i, i ^ 1) for i in range(REQ)]) for o in own]

    sums = list(partial_latents(jnp.stack([y, req % 2]), hidden, own, other))
    sums = sums[:1] + [
        lax.ppermute(sums[m], "req", [(i, i ^ (2 * m)) for i in range(REQ)]) for m in range(1, X)
    ]

    entries = jnp.arange(hit_holder.shape[1], dtype=jnp.int32)
    used = entries[None, :] < hit_count[:, None]
    earlier = (
        (hit_holder[:, :, None] == hit_holder[:, None, :])
        & used[:, None, :]
        & (entries[None, None, :] < entries[None, :, None])
    )
    rank = jnp.sum(earlier.astype(jnp.int32), axis=2)
    cap_ids = jnp.arange(CAP, dtype=jnp.int32)
    pick = (
        used[:, None, :]
        & (hit_holder[:, None, :] == req)
        & (rank[:, None, :] == cap_ids[None, :, None])
    )
    place = jnp.sum(jnp.where(pick, hit_slot[:, None, :], 0), axis=2)
    outgoing = jnp.take(pool[:, 0], place.reshape(-1), axis=0).reshape(REQ, CAP, LAT)
    incoming = lax.all_to_all(outgoing, "req", 0, 0).reshape(REQ * CAP, LAT)
    holder = lax.dynamic_index_in_dim(hit_holder, req, 0, keepdims=False)
    my_rank = lax.dynamic_index_in_dim(rank, req, 0, keepdims=False)
    cached = jnp.take(incoming, holder * CAP + jnp.minimum(my_rank, CAP - 1), axis=0)
    tags = jnp.broadcast_to(
        jnp.eye(8, AUG - LAT, PAGE_LANE - LAT, dtype=cached.dtype), (8, AUG - LAT)
    )
    cached = jnp.concatenate([cached, tags], 1)
    cached, sums[0] = lax.optimization_barrier((cached, sums[0]))
    cached = lax.all_to_all(
        jnp.broadcast_to(cached[None], (Y * Z,) + cached.shape), "ctx", 0, 0
    ).reshape(-1, AUG)

    fresh = finish_keys(info, sums, kv_gain[None], cosine, sine)
    fresh, cached = lax.optimization_barrier((fresh, cached))
    near = lax.all_to_all(fresh, "ctx", 0, 0, axis_index_groups=Z_GROUPS).reshape(-1, AUG)

    far = [lax.ppermute(near, "ctx", y_shift(d)) for d in (1, 3)]

    rows = queries[0].reshape(-1, LAT)
    streamed = pltpu.with_memory_space_constraint(rows, pltpu.HBM)
    carry = attend(info, streamed, None, [near, cached], True, False)
    far, near = lax.optimization_barrier((far, near))
    last = lax.ppermute(near, "ctx", y_shift(2))
    carry = attend(info, rows, carry, far, False, False)
    (out,) = attend(info, rows, carry, [last], False, True)
    return out.reshape(1, TOK, HEADS, VAL)


def solution(mesh):
    in_specs = (
        P("req", "ctx", None),
        P("ctx", None),
        P(),
        P("req", "ctx", None, None),
        P("req", "ctx", None),
        P(),
        P(),
        P(),
    )
    out_specs = P("req", "ctx", None, None)
    return jax.shard_map(shards, mesh=mesh, in_specs=in_specs, out_specs=out_specs, check_vma=False)
```
